32 devices in a mesh: row: 2 (over core), blk: 16 (over z, y, x).
Axes of the slice: x: 2, y: 2, z: 4, core: 2. Of those that a mesh axis runs over, the one named last changes fastest.
Arguments:
- flow_state: float32 [2, 16, 6, 16, 64, 256], P('row', 'blk'), may hold values from -6 to 6
- forcing: float32 [2, 16, 6, 16, 64, 256], P('row', 'blk'), may hold values from -6 to 6
- stiffness: float32 [2, 16, 16, 64, 256], P('row', 'blk'), may hold values from 7 to 14
- advection: float32 [2, 16, 6, 6], P('row', 'blk'), may hold values from -4 to 4
- line_inverse: float32 [2, 16, 96, 96], P('row', 'blk')
- margin_rows: int32 [2, 16, 64, 4], P('row', 'blk'), may hold values from 0 to 67, as said below
- margin_weights: float32 [2, 16, 64, 4], P('row', 'blk'), may hold values from 0 to 1, as said below
- partner_bit: int32 [2, 16], P('row', 'blk'), may hold values from 0 to 2, as said below
- turn_code: int32 [2, 16], P('row', 'blk'), may hold values from 0 to 3, as said below
Outputs:
- final_state: float32 [2, 16, 6, 16, 64, 256], P('row', 'blk')
The draws below stay inside these ranges and needn't reach their ends.
Inputs may be any that keep to these rules, and one draw needn't show every extreme that they name: Within a blade row, blocks 8g to 8g+7 share one value, so that b and b XOR 2**partner_bit[r,b] name each other. `turn_code`: A block and its face partner carry the same code. `margin_rows`: row j of a block reads window rows j to j + 4 only. `margin_weights`: the first 1 to 4 slots of a row carry positive weights summing to one, the others zero.
All inputs are finite; a program needn't handle non-finite values.
Results may differ from the reference program's by a relative error of at most 0.0001.
Values sent between devices are 32-bit elements; how exact they have to be, the bound alone decides.
A program may use at most 128 MiB of HBM per device.

```python
import math
import jax
import jax.numpy as jnp
from jax import lax

NVAR = 6
NI = 16
NJ = 64
NK = 256
OV = 4
HW = 2
SWEEPS = 3
ROWS = 2
NBLK = 16


def pair_groups(key):
    picked = jax.random.randint(jax.random.fold_in(key, 11), (ROWS, NBLK // 8), 0, 3)
    picked = picked.at[0, 0].set(2).at[1, 0].set(0)
    return jnp.repeat(picked, 8, axis=1).astype(jnp.int32)


def margin_layout(key):
    counts = jax.random.randint(jax.random.fold_in(key, 17), (ROWS, NBLK, NJ), 1, OV + 1)
    offsets = jax.random.randint(jax.random.fold_in(key, 19), (ROWS, NBLK, NJ, OV), -HW, HW + 1)
    centre = jnp.arange(NJ, dtype=jnp.int32)[None, None, :, None] + HW
    chosen = centre + offsets
    chosen = chosen.at[:, :, NJ - 1, 0].set(NJ - 1 + 2 * HW).at[:, :, 0, 0].set(0)
    return (counts.astype(jnp.int32), chosen.astype(jnp.int32))


def draw_partner_bit(key, part):
    return pair_groups(key)


def draw_turn_code(key, part):
    levels = pair_groups(key)
    raw_codes = jax.random.randint(jax.random.fold_in(key, 13), (ROWS, NBLK), 0, 4)
    raw_codes = raw_codes.at[0, 0].set(3).at[1, 0].set(0)
    blocks = jnp.arange(NBLK, dtype=jnp.int32)[None, :]
    partner = jnp.bitwise_xor(blocks, jnp.left_shift(jnp.int32(1), levels))
    lowest = jnp.minimum(blocks, partner)
    return jnp.take_along_axis(raw_codes, lowest, axis=1).astype(jnp.int32)


def draw_margin_rows(key, part):
    counts, chosen = margin_layout(key)
    return chosen


def draw_margin_weights(key, part):
    counts, chosen = margin_layout(key)
    raw_weights = jax.random.uniform(jax.random.fold_in(key, 23), (ROWS, NBLK, NJ, OV), jnp.float32, 0.2, 1.0)
    active = jnp.arange(OV, dtype=jnp.int32)[None, None, None, :] < counts[..., None]
    kept = jnp.where(active, raw_weights, 0.0)
    return (kept / jnp.sum(kept, axis=-1, keepdims=True)).astype(jnp.float32)


def draw_line_inverse(key, part):
    order = NVAR * NI
    spread = 0.03 * jax.random.normal(key, (ROWS, NBLK, order, order), jnp.float32)
    identity = jnp.eye(order, dtype=jnp.float32)
    return (0.1 * (identity + spread)).astype(jnp.float32)


def steps_of(stream_key, dims, cuts, low, top_value):
    gain = 1.0
    for dim, shards_of in cuts:
        draws = jax.random.uniform(jax.random.fold_in(jax.random.fold_in(stream_key, 6), dim), (shards_of,), jnp.float32, low / len(cuts), top_value / len(cuts))
        gain = gain * jnp.repeat(jnp.exp(draws), dims[dim] // shards_of).reshape((-1,) + (1,) * (len(dims) - 1 - dim))
    return gain


def scatter_about(rng, dims, scale, reach, split=(), held_as=jnp.bfloat16):
    drawn = scale * jax.random.normal(rng, dims, jnp.float32)
    if split:
        drawn = drawn * steps_of(rng, dims, split, -0.22, 0.18)
    return jnp.clip(drawn, -reach, reach).astype(held_as)


def setup_inputs(seed: int = 0) -> dict:
    keys = jax.random.split(jax.random.key(seed), 10)
    return {
        "flow_state": scatter_about(keys[0], (ROWS, NBLK, NVAR, NI, NJ, NK), 1.0, 6.0, ((0, 2), (1, 16)), jnp.float32),
        "forcing": scatter_about(keys[1], (ROWS, NBLK, NVAR, NI, NJ, NK), 1.0, 6.0, ((0, 2), (1, 16)), jnp.float32),
        "stiffness": jnp.clip(jnp.exp(math.log(14.0) - 0.6931472 * jax.random.uniform(keys[2], (ROWS, NBLK, NI, NJ, NK), jnp.float32) ** steps_of(keys[2], (ROWS, NBLK, NI, NJ, NK), ((0, 2), (1, 16)), -0.2, 0.2)), 7.0, 14.0),
        "advection": scatter_about(keys[3], (ROWS, NBLK, NVAR, NVAR), 0.8, 4.0, ((0, 2), (1, 16)), jnp.float32),
        "line_inverse": draw_line_inverse(jax.random.fold_in(keys[9], 71), 0),
        "margin_rows": draw_margin_rows(jax.random.fold_in(keys[9], 71), 0),
        "margin_weights": draw_margin_weights(jax.random.fold_in(keys[9], 71), 0),
        "partner_bit": draw_partner_bit(jax.random.fold_in(keys[9], 71), 0),
        "turn_code": draw_turn_code(jax.random.fold_in(keys[9], 71), 0),
    }


def orient(surface, turn_code):
    flipped = jnp.flip(surface, -2)
    first = jnp.where((turn_code % 2 == 1)[..., None, None, None], flipped, surface)
    second = jnp.flip(first, -1)
    return jnp.where((turn_code // 2 == 1)[..., None, None, None], second, first)


def blend_matrix(rows_used, weights, extent):
    onehot = (rows_used[..., None] == jnp.arange(extent, dtype=jnp.int32)).astype(jnp.float32)
    return jnp.sum(weights[..., None] * onehot, axis=-2)


def operate(field, forcing, stiffness, advection, inlet_ghost, outlet_ghost, lower_ghost, upper_ghost):
    along_i = jnp.concatenate([inlet_ghost[..., None, :, :], field, outlet_ghost[..., None, :, :]], axis=-3)
    along_j = jnp.concatenate([lower_ghost[..., :, None, :], field, upper_ghost[..., :, None, :]], axis=-2)
    walls = jnp.zeros_like(field[..., :1])
    along_k = jnp.concatenate([walls, field, walls], axis=-1)
    neighbours = along_i[..., 2:, :, :] + along_i[..., :-2, :, :]
    neighbours = neighbours + along_j[..., 2:, :] + along_j[..., :-2, :]
    neighbours = neighbours + along_k[..., 2:] + along_k[..., :-2]
    stretch = along_i[..., 2:, :, :] - along_i[..., :-2, :, :]
    carried = 0.5 * jnp.einsum('...vw,...wijk->...vijk', advection, stretch, precision=lax.Precision.HIGHEST)
    return forcing - (stiffness[..., None, :, :, :] * field - neighbours + carried)


def reference(flow_state, forcing, stiffness, advection, line_inverse, margin_rows, margin_weights, partner_bit, turn_code):
    field = flow_state
    blend = blend_matrix(margin_rows, margin_weights, NJ + 2 * HW)
    row_index = jnp.arange(ROWS, dtype=jnp.int32)[:, None]
    partner = jnp.bitwise_xor(jnp.arange(NBLK, dtype=jnp.int32)[None, :], jnp.left_shift(jnp.int32(1), partner_bit))
    for sweep in range(SWEEPS):
        plane = jnp.stack([field[0, :, :, NI - 1], field[1, :, :, 0]])
        opposite = plane[::-1]
        before = jnp.roll(opposite, 1, axis=1)
        beyond = jnp.roll(opposite, -1, axis=1)
        window = jnp.concatenate([before[..., NJ - HW:, :], opposite, beyond[..., :HW, :]], axis=-2)
        ghosts = jnp.einsum('rbjm,rbvmk->rbvjk', blend, window, precision=lax.Precision.HIGHEST)
        inlet_ghost = jnp.stack([field[0, :, :, 0], ghosts[1]])
        outlet_ghost = jnp.stack([ghosts[0], field[1, :, :, NI - 1]])
        lower_face = field[:, :, :, :, 0, :]
        upper_face = field[:, :, :, :, NJ - 1, :]
        lower_ghost = orient(upper_face[row_index, partner], turn_code)
        upper_ghost = orient(lower_face[row_index, partner], turn_code)
        residue = operate(field, forcing, stiffness, advection, inlet_ghost, outlet_ghost, lower_ghost, upper_ghost)
        flat = residue.reshape((ROWS, NBLK, NVAR * NI, NJ * NK))
        change = jnp.einsum('rbmn,rbnl->rbml', line_inverse, flat, precision=lax.Precision.HIGHEST)
        field = field + change.reshape(field.shape)
    return field
```

```python
import functools

import jax
import jax.numpy as jnp
from jax import lax
from jax.experimental import pallas as pl
from jax.experimental.pallas import tpu as pltpu
from jax.sharding import PartitionSpec as P

HW = 2
SWEEPS = 3
BITS = 3
CHUNK = 8
MESH = pl.DeviceIdType.MESH
EXACT = lax.Precision.HIGHEST


def line_matrix(inverse_ref, jacobian_ref, rotor, nv, ni):
    order = nv * ni
    width = 2 * order + 16
    row = lax.broadcasted_iota(jnp.int32, (order, width), 0)
    col = lax.broadcasted_iota(jnp.int32, (order, width), 1)
    v, i = row // ni, row % ni
    identity = col == row
    in_state = (col >= order) & (col < 2 * order)
    cs = col - order
    w, ic = cs // ni, cs % ni
    ghost = cs - order
    is_ghost = col >= 2 * order
    rotor_m = jnp.broadcast_to(rotor, (order, width))
    top, bottom = i == ni - 1, i == 0
    stator_m = jnp.logical_not(rotor_m)
    up = (in_state & ((ic == i + 1) | (stator_m & top & (ic == ni - 1)))) | (is_ghost & rotor_m & top)
    down = (in_state & ((ic == i - 1) | (rotor_m & bottom & (ic == 0)))) | (
        is_ghost & stator_m & bottom
    )
    upf = jnp.where(up, 1.0, 0.0)
    downf = jnp.where(down, 1.0, 0.0)
    wv = jnp.where(is_ghost, ghost, w)
    coupling = jnp.zeros((order, width), jnp.float32)
    for a in range(nv):
        for b in range(nv):
            coupling = jnp.where((v == a) & (wv == b), jacobian_ref[a, b], coupling)
    same = jnp.where(v == wv, 1.0, 0.0)
    m = jnp.where(identity, 1.0, 0.0) + same * (upf + downf) - 0.5 * coupling * (upf - downf)
    return jnp.dot(inverse_ref[...], m, precision=EXACT, preferred_element_type=jnp.float32)


def kernel(
    nblk,
    nv,
    ni,
    x_hbm,
    f_hbm,
    d_hbm,
    jac,
    inverse,
    mrows,
    mweights,
    pbit,
    tcode,
    out_hbm,
    S,
    F,
    D,
    xs,
    fs,
    ds,
    recv,
    win,
    plane,
    wcat,
    turn_i,
    turn_k,
    coef,
    in_sem,
    out_sem,
    face_send,
    face_recv,
    sis_send,
    sis_recv,
    edge_send,
    edge_recv,
):
    order = nv * ni
    nj, nk = x_hbm.shape[1], x_hbm.shape[2]
    nch = nj // CHUNK
    r = lax.axis_index("row")
    b = lax.axis_index("blk")
    rotor = r == 0
    other = 1 - r
    nxt = lax.rem(b + 1, nblk)
    prv = lax.rem(b + nblk - 1, nblk)
    partners = []
    for bit in range(BITS):
        s = 1 << bit
        partners.append(b + s * (1 - 2 * ((b // s) % 2)))

    def load(which, src, dst, c):
        rows = pl.ds(pl.multiple_of(c * CHUNK, CHUNK), CHUNK)
        return pltpu.make_async_copy(src.at[:, rows, :], dst.at[:, rows, :], in_sem.at[which, c])

    def store(c):
        rows = pl.ds(pl.multiple_of(c * CHUNK, CHUNK), CHUNK)
        return pltpu.make_async_copy(xs.at[:, rows, :], out_hbm.at[:, rows, :], out_sem.at[c])

    for c in [0, nch - 1] + list(range(1, nch - 1)):
        load(0, x_hbm, xs, c).start()
    for c in list(range(2, nch - 2)) + [1, nch - 2, 0, nch - 1]:
        load(1, f_hbm, fs, c).start()
        load(2, d_hbm, ds, c).start()

    barrier = pltpu.get_barrier_semaphore()
    friends = [(other, b), (other, prv), (other, nxt)] + [(r, p) for p in partners]
    for friend in friends:
        pl.semaphore_signal(barrier, inc=1, device_id=friend, device_id_type=MESH)

    wfull = line_matrix(inverse, jac, rotor, nv, ni)
    whi = wfull.astype(jnp.bfloat16)
    wlo = (wfull - whi.astype(jnp.float32)).astype(jnp.bfloat16)
    wcat[0:order, :] = whi
    wcat[order : 2 * order, :] = wlo
    code = tcode[0, 0]
    ra = lax.broadcasted_iota(jnp.int32, (order, order), 0)
    ca = lax.broadcasted_iota(jnp.int32, (order, order), 1)
    turned = ra // ni * ni + (ni - 1 - ra % ni)
    turn_i[...] = jnp.where(ca == jnp.where(code % 2 == 1, turned, ra), 1.0, 0.0)
    rk = lax.broadcasted_iota(jnp.int32, (nk, nk), 0)
    ck = lax.broadcasted_iota(jnp.int32, (nk, nk), 1)
    turn_k[...] = jnp.where(ck == jnp.where(code // 2 == 1, nk - 1 - rk, rk), 1.0, 0.0)

    def coefs(j, carry):
        for d in range(2 * HW + 1):
            total = jnp.float32(0.0)
            for o in range(mrows.shape[1]):
                total = total + jnp.where(mrows[j, o] == j + d, mweights[j, o], 0.0)
            coef[j, d] = total
        return carry

    lax.fori_loop(0, nj, coefs, 0)
    plane[...] = jnp.zeros_like(plane)

    def face(e, bit, f):
        return pltpu.make_async_remote_copy(
            src_ref=S.at[e % 2, 1 if f == 0 else nj],
            dst_ref=recv.at[e, bit, f],
            send_sem=face_send.at[e, bit, f],
            recv_sem=face_recv.at[e, bit, f],
            device_id=(r, partners[bit]),
            device_id_type=MESH,
        )

    def sister(e, c):
        return pltpu.make_async_remote_copy(
            src_ref=plane.at[e, pl.ds(c * CHUNK, CHUNK)],
            dst_ref=win.at[e, pl.ds(HW + c * CHUNK, CHUNK)],
            send_sem=sis_send.at[e, c],
            recv_sem=sis_recv.at[e, c],
            device_id=(other, b),
            device_id_type=MESH,
        )

    def edge(e, f):
        return pltpu.make_async_remote_copy(
            src_ref=plane.at[e, pl.ds(nj - HW if f == 0 else 0, HW)],
            dst_ref=win.at[e, pl.ds(0 if f == 0 else nj + HW, HW)],
            send_sem=edge_send.at[e, f],
            recv_sem=edge_recv.at[e, f],
            device_id=(other, nxt if f == 0 else prv),
            device_id_type=MESH,
        )

    def put_plane(e, j, new):
        for v in range(nv):
            last = new[v * ni + ni - 1 : v * ni + ni]
            first = new[v * ni : v * ni + 1]
            plane[e, j, v : v + 1, :] = jnp.where(rotor, last, first)

    def send_ends(e, f):
        for bit in range(BITS):
            face(e, bit, f).start()
        edge(e, 1 - f).start()

    def take_state(c):
        load(0, x_hbm, xs, c).wait()
        j0 = pl.multiple_of(c * CHUNK, CHUNK)

        def group(g, carry):
            gr = pl.ds(pl.multiple_of(g * 8, 8), 8)
            S[0, pl.ds(j0 + 1, CHUNK), gr, :] = jnp.swapaxes(xs[gr, pl.ds(j0, CHUNK), :], 0, 1)
            return carry

        lax.fori_loop(0, order // 8, group, 0)

        def planes(jj, carry):
            put_plane(0, j0 + jj, S[0, j0 + jj + 1])
            return carry

        lax.fori_loop(0, CHUNK, planes, 0)

    def take_rest(c):
        load(1, f_hbm, fs, c).wait()
        load(2, d_hbm, ds, c).wait()
        j0 = pl.multiple_of(c * CHUNK, CHUNK)

        def group(g, carry):
            gr = pl.ds(pl.multiple_of(g * 8, 8), 8)
            F[pl.ds(j0, CHUNK), gr, :] = jnp.swapaxes(fs[gr, pl.ds(j0, CHUNK), :], 0, 1)
            return carry

        lax.fori_loop(0, order // 8, group, 0)
        for g in range(ni // 8):
            gr = pl.ds(g * 8, 8)
            D[pl.ds(j0, CHUNK), gr, :] = jnp.swapaxes(ds[gr, pl.ds(j0, CHUNK), :], 0, 1)

    take_state(0)
    pl.semaphore_wait(barrier, len(friends))
    sister(0, 0).start()
    send_ends(0, 0)
    take_state(nch - 1)
    sister(0, nch - 1).start()
    send_ends(0, 1)

    def middle(c, carry):
        take_state(c)
        sister(0, c).start()
        return carry

    lax.fori_loop(1, nch - 1, middle, 0)

    lane = lax.broadcasted_iota(jnp.int32, (order, nk), 1)

    def sweep_row(e, j):
        src, dst = e % 2, (e + 1) % 2
        x = S[src, j + 1]
        below = jnp.where(lane == 0, 0.0, pltpu.roll(x, 1, 1))
        above = jnp.where(lane == nk - 1, 0.0, pltpu.roll(x, nk - 1, 1))
        diag = D[j]
        diag = jnp.concatenate([diag] * nv, axis=0)
        near = (S[src, j] + S[src, j + 2]) + (below + above)
        res = F[j] - diag * x + near
        g = coef[j, 0] * win[e, j]
        for d in range(1, 2 * HW + 1):
            g = g + coef[j, d] * win[e, j + d]
        full = jnp.concatenate([res, x, g, jnp.zeros_like(g)], axis=0)
        hi = full.astype(jnp.bfloat16)
        lo = (full - hi.astype(jnp.float32)).astype(jnp.bfloat16)
        o = jnp.dot(wcat[...], hi, preferred_element_type=jnp.float32)
        o2 = jnp.dot(wcat[0:order, :], lo, preferred_element_type=jnp.float32)
        new = x + (o[0:order] + (o[order:] + o2))
        S[dst, j + 1] = new
        if e + 1 < SWEEPS:
            put_plane(e + 1, j, new)

    def do_chunk(e, c):
        if e == 0:
            take_rest(c)
        j0 = c * CHUNK

        def rows(t, carry):
            sweep_row(e, j0 + 2 * t)
            sweep_row(e, j0 + 2 * t + 1)
            return carry

        lax.fori_loop(0, CHUNK // 2, rows, 0)
        if e + 1 < SWEEPS:
            sister(e + 1, c).start()
        else:
            j0 = pl.multiple_of(j0, CHUNK)

            def group(g, carry):
                gr = pl.ds(pl.multiple_of(g * 8, 8), 8)
                xs[gr, pl.ds(j0, CHUNK), :] = jnp.swapaxes(
                    S[(e + 1) % 2, pl.ds(j0 + 1, CHUNK), gr, :], 0, 1
                )
                return carry

            lax.fori_loop(0, order // 8, group, 0)
            store(c).start()

    def ghost_row(e, f):
        picked = recv[e, 0, 1 - f]
        for bit in range(1, BITS):
            picked = jnp.where(pbit[0, 0] == bit, recv[e, bit, 1 - f], picked)
        picked = jnp.dot(picked, turn_k[...], precision=EXACT, preferred_element_type=jnp.float32)
        picked = jnp.dot(turn_i[...], picked, precision=EXACT, preferred_element_type=jnp.float32)
        S[e % 2, 0 if f == 0 else nj + 1] = picked

    for e in range(SWEEPS):
        sister(e, 1).wait_recv()
        sister(e, 2).wait_recv()

        def inner(c, carry):
            sister(e, c + 1).wait_recv()
            do_chunk(e, c)
            return carry

        lax.fori_loop(2, nch - 2, inner, 0)
        sister(e, 0).wait_recv()
        do_chunk(e, 1)
        sister(e, nch - 1).wait_recv()
        do_chunk(e, nch - 2)
        for bit in range(BITS):
            for f in range(2):
                face(e, bit, f).wait()
        for f in range(2):
            edge(e, f).wait()
            ghost_row(e, f)
        do_chunk(e, 0)
        if e + 1 < SWEEPS:
            send_ends(e + 1, 0)
        do_chunk(e, nch - 1)
        if e + 1 < SWEEPS:
            send_ends(e + 1, 1)

        def sent(c, carry):
            sister(e, c).wait_send()
            return carry

        lax.fori_loop(0, nch, sent, 0)

    def finish(c, carry):
        store(c).wait()
        return carry

    lax.fori_loop(0, nch, finish, 0)


def body(nblk, state, forcing, stiffness, advection, inverse, mrows, mweights, pbit, tcode):
    _, _, nv, ni, nj, nk = state.shape
    order = nv * ni
    nch = nj // CHUNK
    f32 = jnp.float32
    anywhere = pl.BlockSpec(memory_space=pl.ANY)
    smem = pl.BlockSpec(memory_space=pltpu.SMEM)
    vmem = pl.BlockSpec(memory_space=pltpu.VMEM)
    dma = pltpu.SemaphoreType.DMA
    out = pl.pallas_call(
        functools.partial(kernel, nblk, nv, ni),
        out_shape=jax.ShapeDtypeStruct((order, nj, nk), f32),
        in_specs=[anywhere] * 3 + [smem, vmem, smem, smem, smem, smem],
        out_specs=anywhere,
        scratch_shapes=[
            pltpu.VMEM((2, nj + 2, order, nk), f32),
            pltpu.VMEM((nj, order, nk), f32),
            pltpu.VMEM((nj, ni, nk), f32),
            pltpu.VMEM((order, nj, nk), f32),
            pltpu.VMEM((order, nj, nk), f32),
            pltpu.VMEM((ni, nj, nk), f32),
            pltpu.VMEM((SWEEPS, BITS, 2, order, nk), f32),
            pltpu.VMEM((SWEEPS, nj + 2 * HW, 8, nk), f32),
            pltpu.VMEM((SWEEPS, nj, 8, nk), f32),
            pltpu.VMEM((2 * order, 2 * order + 16), jnp.bfloat16),
            pltpu.VMEM((order, order), f32),
            pltpu.VMEM((nk, nk), f32),
            pltpu.SMEM((nj, 2 * HW + 1), f32),
            dma((3, nch)),
            dma((nch,)),
            dma((SWEEPS, BITS, 2)),
            dma((SWEEPS, BITS, 2)),
            dma((SWEEPS, nch)),
            dma((SWEEPS, nch)),
            dma((SWEEPS, 2)),
            dma((SWEEPS, 2)),
        ],
        compiler_params=pltpu.CompilerParams(
            collective_id=0, has_side_effects=True, vmem_limit_bytes=56 * 1024 * 1024
        ),
        cost_estimate=pl.CostEstimate(
            flops=SWEEPS * 6 * order * (2 * order + 16) * nj * nk,
            bytes_accessed=4 * (3 * nv + 1) * ni * nj * nk,
            transcendentals=0,
        ),
    )(
        state.reshape(order, nj, nk),
        forcing.reshape(order, nj, nk),
        stiffness.reshape(ni, nj, nk),
        advection[0, 0],
        inverse[0, 0],
        mrows[0, 0],
        mweights[0, 0],
        pbit,
        tcode,
    )
    return out.reshape(state.shape)


def solution(mesh):
    return jax.shard_map(
        functools.partial(body, mesh.shape["blk"]),
        mesh=mesh,
        in_specs=(
            P("row", "blk", None, None, None, None),
            P("row", "blk", None, None, None, None),
            P("row", "blk", None, None, None),
            P("row", "blk", None, None),
            P("row", "blk", None, None),
            P("row", "blk", None, None),
            P("row", "blk", None, None),
            P("row", "blk"),
            P("row", "blk"),
        ),
        out_specs=P("row", "blk", None, None, None, None),
        check_vma=False,
    )
```

```python
import functools

import jax
import jax.numpy as jnp
from jax import lax
from jax.experimental import pallas as pl
from jax.experimental.pallas import tpu as pltpu
from jax.sharding import PartitionSpec as P

HW = 2
SWEEPS = 3
BITS = 3
CHUNK = 8
MESH = pl.DeviceIdType.MESH
EXACT = lax.Precision.HIGHEST


def line_matrix(inverse_ref, jacobian_ref, rotor, nv, ni):
    order = nv * ni
    width = 2 * order + 16
    row = lax.broadcasted_iota(jnp.int32, (order, width), 0)
    col = lax.broadcasted_iota(jnp.int32, (order, width), 1)
    v, i = row // ni, row % ni
    identity = col == row
    in_state = (col >= order) & (col < 2 * order)
    cs = col - order
    w, ic = cs // ni, cs % ni
    ghost = cs - order
    is_ghost = col >= 2 * order
    rotor_m = jnp.broadcast_to(rotor, (order, width))
    top, bottom = i == ni - 1, i == 0
    stator_m = jnp.logical_not(rotor_m)
    up = (in_state & ((ic == i + 1) | (stator_m & top & (ic == ni - 1)))) | (is_ghost & rotor_m & top)
    down = (in_state & ((ic == i - 1) | (rotor_m & bottom & (ic == 0)))) | (
        is_ghost & stator_m & bottom
    )
    upf = jnp.where(up, 1.0, 0.0)
    downf = jnp.where(down, 1.0, 0.0)
    wv = jnp.where(is_ghost, ghost, w)
    coupling = jnp.zeros((order, width), jnp.float32)
    for a in range(nv):
        for b in range(nv):
            coupling = jnp.where((v == a) & (wv == b), jacobian_ref[a, 0, b], coupling)
    same = jnp.where(v == wv, 1.0, 0.0)
    m = jnp.where(identity, 1.0, 0.0) + same * (upf + downf) - 0.5 * coupling * (upf - downf)
    return jnp.dot(inverse_ref[...], m, precision=EXACT, preferred_element_type=jnp.float32)


def kernel(
    nblk,
    nv,
    ni,
    x_hbm,
    f_hbm,
    d_hbm,
    jac,
    inverse,
    mrows,
    mweights,
    pbit,
    tcode,
    out_hbm,
    S0,
    S1,
    F,
    D,
    xs,
    fs,
    ds,
    recv,
    win,
    plane,
    wcat,
    turn_i,
    turn_k,
    coef,
    in_sem,
    out_sem,
    face_send,
    face_recv,
    sis_send,
    sis_recv,
    edge_send,
    edge_recv,
):
    order = nv * ni
    S = (S0, S1)
    nj, nk = x_hbm.shape[1], x_hbm.shape[2]
    nch = nj // CHUNK
    r = lax.axis_index("row")
    b = lax.axis_index("blk")
    rotor = r == 0
    other = 1 - r
    nxt = lax.rem(b + 1, nblk)
    prv = lax.rem(b + nblk - 1, nblk)
    partners = []
    for bit in range(BITS):
        s = 1 << bit
        partners.append(b + s * (1 - 2 * ((b // s) % 2)))

    def load(which, src, dst, c):
        rows = pl.ds(pl.multiple_of(c * CHUNK, CHUNK), CHUNK)
        return pltpu.make_async_copy(src.at[:, rows, :], dst.at[:, rows, :], in_sem.at[which, c])

    def store(c):
        rows = pl.ds(pl.multiple_of(c * CHUNK, CHUNK), CHUNK)
        return pltpu.make_async_copy(xs.at[:, rows, :], out_hbm.at[:, rows, :], out_sem.at[c])

    for c in [0, nch - 1] + list(range(1, nch - 1)):
        load(0, x_hbm, xs, c).start()
    for c in list(range(2, nch - 2)) + [1, nch - 2, 0, nch - 1]:
        load(1, f_hbm, fs, c).start()
        load(2, d_hbm, ds, c).start()

    barrier = pltpu.get_barrier_semaphore()
    friends = [(other, b), (other, prv), (other, nxt)] + [(r, p) for p in partners]
    for friend in friends:
        pl.semaphore_signal(barrier, inc=1, device_id=friend, device_id_type=MESH)

    wfull = line_matrix(inverse, jac, rotor, nv, ni)
    whi = wfull.astype(jnp.bfloat16)
    wlo = (wfull - whi.astype(jnp.float32)).astype(jnp.bfloat16)
    wcat[0:order, :] = whi
    wcat[order : 2 * order, :] = wlo
    code = tcode[0, 0]
    ra = lax.broadcasted_iota(jnp.int32, (order, order), 0)
    ca = lax.broadcasted_iota(jnp.int32, (order, order), 1)
    turned = ra // ni * ni + (ni - 1 - ra % ni)
    chosen = jnp.where(code % 2 == 1, turned, ra)
    turn_i[...] = jnp.where(ca == chosen, 1.0, 0.0).astype(jnp.bfloat16)
    rk = lax.broadcasted_iota(jnp.int32, (nk, nk), 0)
    ck = lax.broadcasted_iota(jnp.int32, (nk, nk), 1)
    chosen_k = jnp.where(code // 2 == 1, nk - 1 - rk, rk)
    turn_k[...] = jnp.where(ck == chosen_k, 1.0, 0.0).astype(jnp.bfloat16)

    def coefs(j, carry):
        for d in range(2 * HW + 1):
            total = jnp.float32(0.0)
            for o in range(mrows.shape[0]):
                total = total + jnp.where(mrows[o, j] == j + d, mweights[o, j], 0.0)
            coef[j, d] = total
        return carry

    lax.fori_loop(0, nj, coefs, 0, unroll=2)
    plane[...] = jnp.zeros_like(plane)

    def face(e, bit, f):
        return pltpu.make_async_remote_copy(
            src_ref=S[e % 2].at[1 if f == 0 else nj],
            dst_ref=recv.at[e, bit, f],
            send_sem=face_send.at[e, bit, f],
            recv_sem=face_recv.at[e, bit, f],
            device_id=(r, partners[bit]),
            device_id_type=MESH,
        )

    def sister(e, c):
        return pltpu.make_async_remote_copy(
            src_ref=plane.at[e, pl.ds(c * CHUNK, CHUNK)],
            dst_ref=win.at[e, pl.ds(HW + c * CHUNK, CHUNK)],
            send_sem=sis_send.at[e, c],
            recv_sem=sis_recv.at[e, c],
            device_id=(other, b),
            device_id_type=MESH,
        )

    def edge(e, f):
        return pltpu.make_async_remote_copy(
            src_ref=plane.at[e, pl.ds(nj - HW if f == 0 else 0, HW)],
            dst_ref=win.at[e, pl.ds(0 if f == 0 else nj + HW, HW)],
            send_sem=edge_send.at[e, f],
            recv_sem=edge_recv.at[e, f],
            device_id=(other, nxt if f == 0 else prv),
            device_id_type=MESH,
        )

    def put_plane(e, j, new):
        for v in range(nv):
            last = new[v * ni + ni - 1 : v * ni + ni]
            first = new[v * ni : v * ni + 1]
            plane[e, j, v : v + 1, :] = jnp.where(rotor, last, first)

    def send_ends(e, f):
        for bit in range(BITS):
            face(e, bit, f).start()
        edge(e, 1 - f).start()

    def take_state(c):
        load(0, x_hbm, xs, c).wait()
        j0 = pl.multiple_of(c * CHUNK, CHUNK)

        def group(g, carry):
            gr = pl.ds(pl.multiple_of(g * 8, 8), 8)
            S0[pl.ds(j0 + 1, CHUNK), gr, :] = jnp.swapaxes(xs[gr, pl.ds(j0, CHUNK), :], 0, 1)
            return carry

        lax.fori_loop(0, order // 8, group, 0, unroll=6)

        for jj in range(CHUNK):
            put_plane(0, j0 + jj, S0[j0 + jj + 1])

    def take_rest(c):
        load(1, f_hbm, fs, c).wait()
        load(2, d_hbm, ds, c).wait()
        j0 = pl.multiple_of(c * CHUNK, CHUNK)

        def group(g, carry):
            gr = pl.ds(pl.multiple_of(g * 8, 8), 8)
            F[pl.ds(j0, CHUNK), gr, :] = jnp.swapaxes(fs[gr, pl.ds(j0, CHUNK), :], 0, 1)
            return carry

        lax.fori_loop(0, order // 8, group, 0, unroll=6)
        for g in range(ni // 8):
            gr = pl.ds(g * 8, 8)
            D[pl.ds(j0, CHUNK), gr, :] = jnp.swapaxes(ds[gr, pl.ds(j0, CHUNK), :], 0, 1)

    take_state(0)
    pl.semaphore_wait(barrier, len(friends))
    sister(0, 0).start()
    send_ends(0, 0)
    take_state(nch - 1)
    sister(0, nch - 1).start()
    send_ends(0, 1)

    def middle(c, carry):
        take_state(c)
        sister(0, c).start()
        return carry

    lax.fori_loop(1, nch - 1, middle, 0)

    lane = lax.broadcasted_iota(jnp.int32, (order, nk), 1)

    def halves(value):
        hi = value.astype(jnp.bfloat16)
        return hi, (value - hi.astype(jnp.float32)).astype(jnp.bfloat16)

    def right_hand(e, j):
        src = S[e % 2]
        x = src[j + 1]
        below = jnp.where(lane == 0, 0.0, pltpu.roll(x, 1, 1))
        above = jnp.where(lane == nk - 1, 0.0, pltpu.roll(x, nk - 1, 1))
        diag = jnp.concatenate([D[j]] * nv, axis=0)
        near = (src[j] + src[j + 2]) + (below + above)
        res = F[j] - diag * x + near
        g = coef[j, 0] * win[e, j]
        for d in range(1, 2 * HW + 1):
            g = g + coef[j, d] * win[e, j + d]
        return halves(jnp.concatenate([res, x, g, jnp.zeros_like(g)], axis=0))

    def do_chunk(e, c):
        if e == 0:
            take_rest(c)
        j0 = c * CHUNK
        src, dst = S[e % 2], S[(e + 1) % 2]
        pairs = [right_hand(e, j0 + t) for t in range(CHUNK)]
        news = []
        for t in range(CHUNK):
            hi, lo = pairs[t]
            o = jnp.dot(wcat[...], hi, preferred_element_type=jnp.float32)
            o2 = jnp.dot(wcat[0:order, :], lo, preferred_element_type=jnp.float32)
            news.append(src[j0 + t + 1] + (o[0:order] + (o[order:] + o2)))
        for t in range(CHUNK):
            dst[j0 + t + 1] = news[t]
            if e + 1 < SWEEPS:
                put_plane(e + 1, j0 + t, news[t])
        if e + 1 < SWEEPS:
            sister(e + 1, c).start()
        else:
            j0 = pl.multiple_of(j0, CHUNK)

            def group(g, carry):
                gr = pl.ds(pl.multiple_of(g * 8, 8), 8)
                xs[gr, pl.ds(j0, CHUNK), :] = jnp.swapaxes(
                    dst[pl.ds(j0 + 1, CHUNK), gr, :], 0, 1
                )
                return carry

            lax.fori_loop(0, order // 8, group, 0, unroll=6)
            store(c).start()

    def ghost_row(e, f):
        picked = recv[e, 0, 1 - f]
        for bit in range(1, BITS):
            picked = jnp.where(pbit[0, 0] == bit, recv[e, bit, 1 - f], picked)
        both = jnp.concatenate(halves(picked), axis=0)
        both = jnp.dot(both, turn_k[...], preferred_element_type=jnp.float32)
        parts = both.astype(jnp.bfloat16)
        swap = turn_i[...]
        first = jnp.dot(swap, parts[0:order], preferred_element_type=jnp.float32)
        second = jnp.dot(swap, parts[order:], preferred_element_type=jnp.float32)
        S[e % 2][0 if f == 0 else nj + 1] = first + second

    for e in range(SWEEPS):
        sister(e, 1).wait_recv()
        sister(e, 2).wait_recv()

        def step(pos, carry):
            c = jnp.where(
                pos < nch - 4,
                pos + 2,
                jnp.where(
                    pos < nch - 2,
                    1 + (pos - (nch - 4)) * (nch - 3),
                    (pos - (nch - 2)) * (nch - 1),
                ),
            )

            @pl.when(pos < nch - 4)
            def _():
                sister(e, pos + 3).wait_recv()

            @pl.when(pos == nch - 4)
            def _():
                sister(e, 0).wait_recv()

            @pl.when(pos == nch - 3)
            def _():
                sister(e, nch - 1).wait_recv()

            @pl.when(pos == nch - 2)
            def _():
                for f in range(2):
                    for bit in range(BITS):
                        face(e, bit, f).wait()
                    edge(e, f).wait()
                for f in range(2):
                    ghost_row(e, f)

            do_chunk(e, c)
            if e + 1 < SWEEPS:
                for f in range(2):

                    @pl.when(pos == nch - 2 + f)
                    def _():
                        send_ends(e + 1, f)

            return carry

        lax.fori_loop(0, nch, step, 0)

        def sent(c, carry):
            sister(e, c).wait_send()
            return carry

        lax.fori_loop(0, nch, sent, 0)

    def finish(c, carry):
        store(c).wait()
        return carry

    lax.fori_loop(0, nch, finish, 0)


def body(nblk, state, forcing, stiffness, advection, inverse, mrows, mweights, pbit, tcode):
    _, _, nv, ni, nj, nk = state.shape
    order = nv * ni
    nch = nj // CHUNK
    f32 = jnp.float32
    anywhere = pl.BlockSpec(memory_space=pl.ANY)
    smem = pl.BlockSpec(memory_space=pltpu.SMEM)
    vmem = pl.BlockSpec(memory_space=pltpu.VMEM)
    dma = pltpu.SemaphoreType.DMA
    out = pl.pallas_call(
        functools.partial(kernel, nblk, nv, ni),
        out_shape=jax.ShapeDtypeStruct((order, nj, nk), f32),
        in_specs=[anywhere] * 3 + [smem, vmem, smem, smem, smem, smem],
        out_specs=anywhere,
        scratch_shapes=[
            pltpu.VMEM((nj + 2, order, nk), f32),
            pltpu.VMEM((nj + 2, order, nk), f32),
            pltpu.VMEM((nj, order, nk), f32),
            pltpu.VMEM((nj, ni, nk), f32),
            pltpu.VMEM((order, nj, nk), f32),
            pltpu.VMEM((order, nj, nk), f32),
            pltpu.VMEM((ni, nj, nk), f32),
            pltpu.VMEM((SWEEPS, BITS, 2, order, nk), f32),
            pltpu.VMEM((SWEEPS, nj + 2 * HW, 8, nk), f32),
            pltpu.VMEM((SWEEPS, nj, 8, nk), f32),
            pltpu.VMEM((2 * order, 2 * order + 16), jnp.bfloat16),
            pltpu.VMEM((order, order), jnp.bfloat16),
            pltpu.VMEM((nk, nk), jnp.bfloat16),
            pltpu.SMEM((nj, 2 * HW + 1), f32),
            dma((3, nch)),
            dma((nch,)),
            dma((SWEEPS, BITS, 2)),
            dma((SWEEPS, BITS, 2)),
            dma((SWEEPS, nch)),
            dma((SWEEPS, nch)),
            dma((SWEEPS, 2)),
            dma((SWEEPS, 2)),
        ],
        compiler_params=pltpu.CompilerParams(
            collective_id=0, has_side_effects=True, vmem_limit_bytes=56 * 1024 * 1024
        ),
        cost_estimate=pl.CostEstimate(
            flops=SWEEPS * 6 * order * (2 * order + 16) * nj * nk,
            bytes_accessed=4 * (3 * nv + 1) * ni * nj * nk,
            transcendentals=0,
        ),
    )(
        state.reshape(order, nj, nk),
        forcing.reshape(order, nj, nk),
        stiffness.reshape(ni, nj, nk),
        advection.transpose(0, 2, 1, 3)[0],
        inverse[0, 0],
        mrows[0, 0].T,
        mweights[0, 0].T,
        pbit,
        tcode,
    )
    return out.reshape(state.shape)


def solution(mesh):
    return jax.shard_map(
        functools.partial(body, mesh.shape["blk"]),
        mesh=mesh,
        in_specs=(
            P("row", "blk", None, None, None, None),
            P("row", "blk", None, None, None, None),
            P("row", "blk", None, None, None),
            P("row", "blk", None, None),
            P("row", "blk", None, None),
            P("row", "blk", None, None),
            P("row", "blk", None, None),
            P("row", "blk"),
            P("row", "blk"),
        ),
        out_specs=P("row", "blk", None, None, None, None),
        check_vma=False,
    )
```

```python
import functools

import jax
import jax.numpy as jnp
from jax import lax
from jax.experimental import pallas as pl
from jax.experimental.pallas import tpu as pltpu
from jax.sharding import PartitionSpec as P

HW = 2
SWEEPS = 3
BITS = 3
CHUNK = 8
MESH = pl.DeviceIdType.MESH
EXACT = lax.Precision.HIGHEST


def line_matrix(inverse_ref, jacobian_ref, rotor, nv, ni):
    order = nv * ni
    width = 2 * order + 16
    row = lax.broadcasted_iota(jnp.int32, (order, width), 0)
    col = lax.broadcasted_iota(jnp.int32, (order, width), 1)
    v, i = row // ni, row % ni
    identity = col == row
    in_state = (col >= order) & (col < 2 * order)
    cs = col - order
    w, ic = cs // ni, cs % ni
    ghost = cs - order
    is_ghost = col >= 2 * order
    rotor_m = jnp.broadcast_to(rotor, (order, width))
    top, bottom = i == ni - 1, i == 0
    stator_m = jnp.logical_not(rotor_m)
    up = (in_state & ((ic == i + 1) | (stator_m & top & (ic == ni - 1)))) | (is_ghost & rotor_m & top)
    down = (in_state & ((ic == i - 1) | (rotor_m & bottom & (ic == 0)))) | (
        is_ghost & stator_m & bottom
    )
    upf = jnp.where(up, 1.0, 0.0)
    downf = jnp.where(down, 1.0, 0.0)
    wv = jnp.where(is_ghost, ghost, w)
    coupling = jnp.zeros((order, width), jnp.float32)
    for a in range(nv):
        for b in range(nv):
            coupling = jnp.where((v == a) & (wv == b), jacobian_ref[a, 0, b], coupling)
    same = jnp.where(v == wv, 1.0, 0.0)
    m = jnp.where(identity, 1.0, 0.0) + same * (upf + downf) - 0.5 * coupling * (upf - downf)
    return jnp.dot(inverse_ref[...], m, precision=EXACT, preferred_element_type=jnp.float32)


def kernel(
    nblk,
    nv,
    ni,
    x_hbm,
    f_hbm,
    d_hbm,
    jac,
    inverse,
    mrows,
    mweights,
    pbit,
    tcode,
    out_hbm,
    S0,
    S1,
    F,
    D,
    xs,
    fs,
    ds,
    recv,
    win,
    plane,
    wcat,
    turn_i,
    turn_k,
    coef,
    RH0,
    RH1,
    RL0,
    RL1,
    in_sem,
    out_sem,
    face_send,
    face_recv,
    sis_send,
    sis_recv,
    edge_send,
    edge_recv,
):
    order = nv * ni
    S, RH, RL = (S0, S1), (RH0, RH1), (RL0, RL1)
    nj, nk = x_hbm.shape[1], x_hbm.shape[2]
    nch = nj // CHUNK
    r = lax.axis_index("row")
    b = lax.axis_index("blk")
    rotor = r == 0
    other = 1 - r
    nxt = lax.rem(b + 1, nblk)
    prv = lax.rem(b + nblk - 1, nblk)
    partners = []
    for bit in range(BITS):
        s = 1 << bit
        partners.append(b + s * (1 - 2 * ((b // s) % 2)))

    def load(which, src, dst, c):
        rows = pl.ds(pl.multiple_of(c * CHUNK, CHUNK), CHUNK)
        return pltpu.make_async_copy(src.at[:, rows, :], dst.at[:, rows, :], in_sem.at[which, c])

    def store(c):
        rows = pl.ds(pl.multiple_of(c * CHUNK, CHUNK), CHUNK)
        return pltpu.make_async_copy(xs.at[:, rows, :], out_hbm.at[:, rows, :], out_sem.at[c])

    for c in [0, nch - 1] + list(range(1, nch - 1)):
        load(0, x_hbm, xs, c).start()
    for c in list(range(2, nch - 2)) + [1, nch - 2, 0, nch - 1]:
        load(1, f_hbm, fs, c).start()
        load(2, d_hbm, ds, c).start()

    barrier = pltpu.get_barrier_semaphore()
    friends = [(other, b), (other, prv), (other, nxt)] + [(r, p) for p in partners]
    for friend in friends:
        pl.semaphore_signal(barrier, inc=1, device_id=friend, device_id_type=MESH)

    wfull = line_matrix(inverse, jac, rotor, nv, ni)
    whi = wfull.astype(jnp.bfloat16)
    wlo = (wfull - whi.astype(jnp.float32)).astype(jnp.bfloat16)
    wcat[0:order, :] = whi
    wcat[order : 2 * order, :] = wlo
    code = tcode[0, 0]
    ra = lax.broadcasted_iota(jnp.int32, (order, order), 0)
    ca = lax.broadcasted_iota(jnp.int32, (order, order), 1)
    turned = ra // ni * ni + (ni - 1 - ra % ni)
    chosen = jnp.where(code % 2 == 1, turned, ra)
    turn_i[...] = jnp.where(ca == chosen, 1.0, 0.0).astype(jnp.bfloat16)
    rk = lax.broadcasted_iota(jnp.int32, (nk, nk), 0)
    ck = lax.broadcasted_iota(jnp.int32, (nk, nk), 1)
    chosen_k = jnp.where(code // 2 == 1, nk - 1 - rk, rk)
    turn_k[...] = jnp.where(ck == chosen_k, 1.0, 0.0).astype(jnp.bfloat16)

    plane[...] = jnp.zeros_like(plane)

    def face(e, bit, f):
        return pltpu.make_async_remote_copy(
            src_ref=S[e % 2].at[1 if f == 0 else nj],
            dst_ref=recv.at[e, bit, f],
            send_sem=face_send.at[e, bit, f],
            recv_sem=face_recv.at[e, bit, f],
            device_id=(r, partners[bit]),
            device_id_type=MESH,
        )

    def sister(e, c):
        return pltpu.make_async_remote_copy(
            src_ref=plane.at[e, pl.ds(c * CHUNK, CHUNK)],
            dst_ref=win.at[e, pl.ds(HW + c * CHUNK, CHUNK)],
            send_sem=sis_send.at[e, c],
            recv_sem=sis_recv.at[e, c],
            device_id=(other, b),
            device_id_type=MESH,
        )

    def edge(e, f):
        return pltpu.make_async_remote_copy(
            src_ref=plane.at[e, pl.ds(nj - HW if f == 0 else 0, HW)],
            dst_ref=win.at[e, pl.ds(0 if f == 0 else nj + HW, HW)],
            send_sem=edge_send.at[e, f],
            recv_sem=edge_recv.at[e, f],
            device_id=(other, nxt if f == 0 else prv),
            device_id_type=MESH,
        )

    def put_plane(e, j, new):
        for v in range(nv):
            last = new[v * ni + ni - 1 : v * ni + ni]
            first = new[v * ni : v * ni + 1]
            plane[e, j, v : v + 1, :] = jnp.where(rotor, last, first)

    def send_ends(e, f):
        for bit in range(BITS):
            face(e, bit, f).start()
        edge(e, 1 - f).start()

    def take_state(c):
        load(0, x_hbm, xs, c).wait()
        j0 = pl.multiple_of(c * CHUNK, CHUNK)

        def group(g, carry):
            gr = pl.ds(pl.multiple_of(g * 8, 8), 8)
            S0[pl.ds(j0 + 1, CHUNK), gr, :] = jnp.swapaxes(xs[gr, pl.ds(j0, CHUNK), :], 0, 1)
            return carry

        lax.fori_loop(0, order // 8, group, 0, unroll=6)

        for jj in range(CHUNK):
            put_plane(0, j0 + jj, S0[j0 + jj + 1])

    take_state(0)
    pl.semaphore_wait(barrier, len(friends))
    sister(0, 0).start()
    send_ends(0, 0)
    take_state(nch - 1)
    sister(0, nch - 1).start()
    send_ends(0, 1)

    def middle(c, carry):
        take_state(c)
        sister(0, c).start()
        return carry

    lax.fori_loop(1, nch - 1, middle, 0)

    lane = lax.broadcasted_iota(jnp.int32, (order, 128), 1)

    def halves(value):
        hi = value.astype(jnp.bfloat16)
        return hi, (value - hi.astype(jnp.float32)).astype(jnp.bfloat16)

    def span_sum(x):
        tiles = [x[:, t : t + 128] for t in range(0, nk, 128)]
        after = [pltpu.roll(t, 1, 1) for t in tiles]
        ahead = [pltpu.roll(t, 127, 1) for t in tiles]
        sums = []
        for t in range(len(tiles)):
            from_left = after[t - 1] if t else 0.0
            from_right = ahead[t + 1] if t + 1 < len(tiles) else 0.0
            below = jnp.where(lane == 0, from_left, after[t])
            above = jnp.where(lane == 127, from_right, ahead[t])
            sums.append(below + above)
        return jnp.concatenate(sums, axis=1)

    def right_hand(e, j):
        src = S[e % 2]
        x = src[j + 1]
        diag = jnp.concatenate([D[j]] * nv, axis=0)
        near = (src[j] + src[j + 2]) + span_sum(x)
        res = F[j] - diag * x + near
        g = None
        for d in range(2 * HW + 1):
            if e == 0:
                c = jnp.float32(0.0)
                for o in range(mrows.shape[0]):
                    c = c + jnp.where(mrows[o, j] == j + d, mweights[o, j], 0.0)
                coef[j, d] = c
            else:
                c = coef[j, d]
            term = c * win[e, j + d]
            g = term if g is None else g + term
        return halves(jnp.concatenate([res, x, g, jnp.zeros_like(g)], axis=0))

    def wait_rest(c):
        load(1, f_hbm, fs, c).wait()
        load(2, d_hbm, ds, c).wait()

    def take_rest(c):
        rows = pl.ds(pl.multiple_of(c * CHUNK, CHUNK), CHUNK)
        for g in range(order // 8):
            gr = pl.ds(g * 8, 8)
            F[rows, gr, :] = jnp.swapaxes(fs[gr, rows, :], 0, 1)
        for g in range(ni // 8):
            gr = pl.ds(g * 8, 8)
            D[rows, gr, :] = jnp.swapaxes(ds[gr, rows, :], 0, 1)

    def advance(now, later):
        if later is not None and later[0] == 0:
            take_rest(later[1])
        news = []
        for t in range(CHUNK):
            if later is not None:
                e, c, slot = later
                hi, lo = right_hand(e, c * CHUNK + t)
                RH[slot][t] = hi
                RL[slot][t] = lo
            if now is not None:
                e, c, slot = now
                j = c * CHUNK + t
                o = jnp.dot(wcat[...], RH[slot][t], preferred_element_type=jnp.float32)
                o2 = jnp.dot(wcat[0:order, :], RL[slot][t], preferred_element_type=jnp.float32)
                new = S[e % 2][j + 1] + (o[0:order] + (o[order:] + o2))
                if e + 1 < SWEEPS:
                    S[(e + 1) % 2][j + 1] = new
                    put_plane(e + 1, j, new)
                else:
                    news.append(new)
        if now is None:
            return
        e, c, slot = now
        if e + 1 < SWEEPS:
            sister(e + 1, c).start()
        else:
            rows = pl.ds(pl.multiple_of(c * CHUNK, CHUNK), CHUNK)
            for g in range(0, order, 8):
                block = jnp.stack([new[g : g + 8] for new in news])
                xs[g : g + 8, rows, :] = jnp.swapaxes(block, 0, 1)
            store(c).start()

    def ghost_row(e, f):
        picked = recv[e, 0, 1 - f]
        for bit in range(1, BITS):
            picked = jnp.where(pbit[0, 0] == bit, recv[e, bit, 1 - f], picked)
        both = jnp.concatenate(halves(picked), axis=0)
        both = jnp.dot(both, turn_k[...], preferred_element_type=jnp.float32)
        parts = both.astype(jnp.bfloat16)
        swap = turn_i[...]
        first = jnp.dot(swap, parts[0:order], preferred_element_type=jnp.float32)
        second = jnp.dot(swap, parts[order:], preferred_element_type=jnp.float32)
        S[e % 2][0 if f == 0 else nj + 1] = first + second

    def chunk_at(pos):
        return jnp.where(
            pos < nch - 4,
            pos + 2,
            jnp.where(pos < nch - 3, 1, jnp.where(pos < nch - 2, nch - 2, 0)),
        )

    def ready(e, pos):
        @pl.when(pos < nch - 4)
        def _():
            sister(e, pos + 3).wait_recv()

        @pl.when(pos == nch - 4)
        def _():
            sister(e, 0).wait_recv()

        @pl.when(pos == nch - 3)
        def _():
            sister(e, nch - 1).wait_recv()

        @pl.when(pos == nch - 2)
        def _():
            for f in range(2):
                for bit in range(BITS):
                    face(e, bit, f).wait()
                edge(e, f).wait()
            for f in range(2):
                ghost_row(e, f)

        if e == 0:
            wait_rest(chunk_at(pos))

    def first_ready(e):
        for c in (1, 2, 3):
            sister(e, c).wait_recv()
        if e == 0:
            wait_rest(2)

    first_ready(0)
    advance(None, (0, 2, 0))
    for e in range(SWEEPS):

        def two(it, carry):
            for half in range(2):
                pos = 2 * it + half
                ready(e, pos + 1)
                advance((e, chunk_at(pos), half), (e, chunk_at(pos + 1), 1 - half))
            return carry

        lax.fori_loop(0, nch // 2 - 1, two, 0)
        if e == 0:
            wait_rest(nch - 1)
        advance((e, 0, 0), (e, nch - 1, 1))
        if e + 1 < SWEEPS:
            send_ends(e + 1, 0)
            first_ready(e + 1)
            advance((e, nch - 1, 1), (e + 1, 2, 0))
            send_ends(e + 1, 1)
        else:
            advance((e, nch - 1, 1), None)

        def sent(c, carry):
            sister(e, c).wait_send()
            return carry

        lax.fori_loop(0, nch, sent, 0)

    def finish(c, carry):
        store(c).wait()
        return carry

    lax.fori_loop(0, nch, finish, 0)


def body(nblk, state, forcing, stiffness, advection, inverse, mrows, mweights, pbit, tcode):
    _, _, nv, ni, nj, nk = state.shape
    order = nv * ni
    nch = nj // CHUNK
    f32 = jnp.float32
    anywhere = pl.BlockSpec(memory_space=pl.ANY)
    smem = pl.BlockSpec(memory_space=pltpu.SMEM)
    vmem = pl.BlockSpec(memory_space=pltpu.VMEM)
    dma = pltpu.SemaphoreType.DMA
    out = pl.pallas_call(
        functools.partial(kernel, nblk, nv, ni),
        out_shape=jax.ShapeDtypeStruct((order, nj, nk), f32),
        in_specs=[anywhere] * 3 + [smem, vmem, smem, smem, smem, smem],
        out_specs=anywhere,
        scratch_shapes=[
            pltpu.VMEM((nj + 2, order, nk), f32),
            pltpu.VMEM((nj + 2, order, nk), f32),
            pltpu.VMEM((nj, order, nk), f32),
            pltpu.VMEM((nj, ni, nk), f32),
            pltpu.VMEM((order, nj, nk), f32),
            pltpu.VMEM((order, nj, nk), f32),
            pltpu.VMEM((ni, nj, nk), f32),
            pltpu.VMEM((SWEEPS, BITS, 2, order, nk), f32),
            pltpu.VMEM((SWEEPS, nj + 2 * HW, 8, nk), f32),
            pltpu.VMEM((SWEEPS, nj, 8, nk), f32),
            pltpu.VMEM((2 * order, 2 * order + 16), jnp.bfloat16),
            pltpu.VMEM((order, order), jnp.bfloat16),
            pltpu.VMEM((nk, nk), jnp.bfloat16),
            pltpu.SMEM((nj, 2 * HW + 1), f32),
        ]
        + [pltpu.VMEM((CHUNK, 2 * order + 16, nk), jnp.bfloat16)] * 4
        + [
            dma((3, nch)),
            dma((nch,)),
            dma((SWEEPS, BITS, 2)),
            dma((SWEEPS, BITS, 2)),
            dma((SWEEPS, nch)),
            dma((SWEEPS, nch)),
            dma((SWEEPS, 2)),
            dma((SWEEPS, 2)),
        ],
        compiler_params=pltpu.CompilerParams(
            collective_id=0, has_side_effects=True, vmem_limit_bytes=56 * 1024 * 1024
        ),
        cost_estimate=pl.CostEstimate(
            flops=SWEEPS * 6 * order * (2 * order + 16) * nj * nk,
            bytes_accessed=4 * (3 * nv + 1) * ni * nj * nk,
            transcendentals=0,
        ),
    )(
        state.reshape(order, nj, nk),
        forcing.reshape(order, nj, nk),
        stiffness.reshape(ni, nj, nk),
        advection.transpose(0, 2, 1, 3)[0],
        inverse[0, 0],
        mrows[0, 0].T,
        mweights[0, 0].T,
        pbit,
        tcode,
    )
    return out.reshape(state.shape)


def solution(mesh):
    return jax.shard_map(
        functools.partial(body, mesh.shape["blk"]),
        mesh=mesh,
        in_specs=(
            P("row", "blk", None, None, None, None),
            P("row", "blk", None, None, None, None),
            P("row", "blk", None, None, None),
            P("row", "blk", None, None),
            P("row", "blk", None, None),
            P("row", "blk", None, None),
            P("row", "blk", None, None),
            P("row", "blk"),
            P("row", "blk"),
        ),
        out_specs=P("row", "blk", None, None, None, None),
        check_vma=False,
    )
```

```python
import functools

import jax
import jax.numpy as jnp
from jax import lax
from jax.experimental import pallas as pl
from jax.experimental.pallas import tpu as pltpu
from jax.sharding import PartitionSpec as P

HW = 2
SWEEPS = 3
BITS = 3
CHUNK = 8
MESH = pl.DeviceIdType.MESH
EXACT = lax.Precision.HIGHEST


def line_matrix(inverse_ref, jacobian_ref, rotor, nv, ni):
    order = nv * ni
    width = 2 * order + 16
    row = lax.broadcasted_iota(jnp.int32, (order, width), 0)
    col = lax.broadcasted_iota(jnp.int32, (order, width), 1)
    v, i = row // ni, row % ni
    identity = col == row
    in_state = (col >= order) & (col < 2 * order)
    cs = col - order
    w, ic = cs // ni, cs % ni
    ghost = cs - order
    is_ghost = col >= 2 * order
    rotor_m = jnp.broadcast_to(rotor, (order, width))
    top, bottom = i == ni - 1, i == 0
    stator_m = jnp.logical_not(rotor_m)
    up = (in_state & ((ic == i + 1) | (stator_m & top & (ic == ni - 1)))) | (is_ghost & rotor_m & top)
    down = (in_state & ((ic == i - 1) | (rotor_m & bottom & (ic == 0)))) | (
        is_ghost & stator_m & bottom
    )
    upf = jnp.where(up, 1.0, 0.0)
    downf = jnp.where(down, 1.0, 0.0)
    wv = jnp.where(is_ghost, ghost, w)
    coupling = jnp.zeros((order, width), jnp.float32)
    for a in range(nv):
        for b in range(nv):
            coupling = jnp.where((v == a) & (wv == b), jacobian_ref[a, 0, b], coupling)
    same = jnp.where(v == wv, 1.0, 0.0)
    m = jnp.where(identity, 1.0, 0.0) + same * (upf + downf) - 0.5 * coupling * (upf - downf)
    return jnp.dot(inverse_ref[...], m, precision=EXACT, preferred_element_type=jnp.float32)


def kernel(
    nblk,
    nv,
    ni,
    x_hbm,
    f_hbm,
    d_hbm,
    jac,
    inverse,
    mrows,
    mweights,
    pbit,
    tcode,
    out_hbm,
    S0,
    S1,
    F,
    D,
    xs,
    fs,
    ds,
    recv,
    win,
    plane,
    wcat,
    turn_i,
    turn_k,
    coef,
    RH0,
    RH1,
    RL0,
    RL1,
    in_sem,
    out_sem,
    face_send,
    face_recv,
    sis_send,
    sis_recv,
    edge_send,
    edge_recv,
):
    order = nv * ni
    S, RH, RL = (S0, S1), (RH0, RH1), (RL0, RL1)
    nj, nk = x_hbm.shape[1], x_hbm.shape[2]
    nch = nj // CHUNK
    r = lax.axis_index("row")
    b = lax.axis_index("blk")
    rotor = r == 0
    other = 1 - r
    nxt = lax.rem(b + 1, nblk)
    prv = lax.rem(b + nblk - 1, nblk)
    partners = []
    for bit in range(BITS):
        s = 1 << bit
        partners.append(b + s * (1 - 2 * ((b // s) % 2)))

    def load(which, src, dst, c):
        rows = pl.ds(pl.multiple_of(c * CHUNK, CHUNK), CHUNK)
        return pltpu.make_async_copy(src.at[:, rows, :], dst.at[:, rows, :], in_sem.at[which, c])

    def store(c):
        rows = pl.ds(pl.multiple_of(c * CHUNK, CHUNK), CHUNK)
        return pltpu.make_async_copy(xs.at[:, rows, :], out_hbm.at[:, rows, :], out_sem.at[c])

    for c in [0, nch - 1] + list(range(1, nch - 1)):
        load(0, x_hbm, xs, c).start()
    for c in list(range(2, nch - 2)) + [1, nch - 2, 0, nch - 1]:
        load(1, f_hbm, fs, c).start()
        load(2, d_hbm, ds, c).start()

    barrier = pltpu.get_barrier_semaphore()
    friends = [(other, b), (other, prv), (other, nxt)] + [(r, p) for p in partners]
    for friend in friends:
        pl.semaphore_signal(barrier, inc=1, device_id=friend, device_id_type=MESH)

    wfull = line_matrix(inverse, jac, rotor, nv, ni)
    whi = wfull.astype(jnp.bfloat16)
    wlo = (wfull - whi.astype(jnp.float32)).astype(jnp.bfloat16)
    wcat[0:order, :] = whi
    wcat[order : 2 * order, :] = wlo
    code = tcode[0, 0]
    ra = lax.broadcasted_iota(jnp.int32, (order, order), 0)
    ca = lax.broadcasted_iota(jnp.int32, (order, order), 1)
    turned = ra // ni * ni + (ni - 1 - ra % ni)
    chosen = jnp.where(code % 2 == 1, turned, ra)
    turn_i[...] = jnp.where(ca == chosen, 1.0, 0.0).astype(jnp.bfloat16)
    rk = lax.broadcasted_iota(jnp.int32, (nk, nk), 0)
    ck = lax.broadcasted_iota(jnp.int32, (nk, nk), 1)
    chosen_k = jnp.where(code // 2 == 1, nk - 1 - rk, rk)
    turn_k[...] = jnp.where(ck == chosen_k, 1.0, 0.0).astype(jnp.bfloat16)

    plane[...] = jnp.zeros_like(plane)

    def face(e, bit, f, first=0, count=None):
        lines = pl.ds(first, order if count is None else count)
        return pltpu.make_async_remote_copy(
            src_ref=S[e % 2].at[1 if f == 0 else nj, lines],
            dst_ref=recv.at[e, bit, f, lines],
            send_sem=face_send.at[e, bit, f],
            recv_sem=face_recv.at[e, bit, f],
            device_id=(r, partners[bit]),
            device_id_type=MESH,
        )

    def sister(e, c):
        return pltpu.make_async_remote_copy(
            src_ref=plane.at[e, pl.ds(c * CHUNK, CHUNK)],
            dst_ref=win.at[e, pl.ds(HW + c * CHUNK, CHUNK)],
            send_sem=sis_send.at[e, c],
            recv_sem=sis_recv.at[e, c],
            device_id=(other, b),
            device_id_type=MESH,
        )

    def edge(e, f):
        return pltpu.make_async_remote_copy(
            src_ref=plane.at[e, pl.ds(nj - HW if f == 0 else 0, HW)],
            dst_ref=win.at[e, pl.ds(0 if f == 0 else nj + HW, HW)],
            send_sem=edge_send.at[e, f],
            recv_sem=edge_recv.at[e, f],
            device_id=(other, nxt if f == 0 else prv),
            device_id_type=MESH,
        )

    def put_plane(e, j, new):
        for v in range(nv):
            last = new[v * ni + ni - 1 : v * ni + ni]
            first = new[v * ni : v * ni + 1]
            plane[e, j, v : v + 1, :] = jnp.where(rotor, last, first)

    def send_ends(e, f):
        edge(e, 1 - f).start()
        for first in range(0, order, 24):
            for bit in range(BITS):
                face(e, bit, f, first, 24).start()

    def take_state(c):
        load(0, x_hbm, xs, c).wait()
        j0 = pl.multiple_of(c * CHUNK, CHUNK)

        def group(g, carry):
            gr = pl.ds(pl.multiple_of(g * 8, 8), 8)
            S0[pl.ds(j0 + 1, CHUNK), gr, :] = jnp.swapaxes(xs[gr, pl.ds(j0, CHUNK), :], 0, 1)
            return carry

        lax.fori_loop(0, order // 8, group, 0, unroll=6)

        for jj in range(CHUNK):
            put_plane(0, j0 + jj, S0[j0 + jj + 1])

    take_state(0)
    pl.semaphore_wait(barrier, len(friends))
    sister(0, 0).start()
    send_ends(0, 0)
    take_state(nch - 1)
    sister(0, nch - 1).start()
    send_ends(0, 1)

    def middle(c, carry):
        take_state(c)
        sister(0, c).start()
        return carry

    lax.fori_loop(1, nch - 1, middle, 0)

    lane = lax.broadcasted_iota(jnp.int32, (order, 128), 1)

    def halves(value):
        hi = value.astype(jnp.bfloat16)
        return hi, (value - hi.astype(jnp.float32)).astype(jnp.bfloat16)

    def span_sum(x):
        tiles = [x[:, t : t + 128] for t in range(0, nk, 128)]
        after = [pltpu.roll(t, 1, 1) for t in tiles]
        ahead = [pltpu.roll(t, 127, 1) for t in tiles]
        sums = []
        for t in range(len(tiles)):
            from_left = after[t - 1] if t else 0.0
            from_right = ahead[t + 1] if t + 1 < len(tiles) else 0.0
            below = jnp.where(lane == 0, from_left, after[t])
            above = jnp.where(lane == 127, from_right, ahead[t])
            sums.append(below + above)
        return jnp.concatenate(sums, axis=1)

    def right_hand(e, j):
        src = S[e % 2]
        x = src[j + 1]
        diag = jnp.concatenate([D[j]] * nv, axis=0)
        near = (src[j] + src[j + 2]) + span_sum(x)
        res = F[j] - diag * x + near
        g = None
        for d in range(2 * HW + 1):
            if e == 0:
                c = jnp.float32(0.0)
                for o in range(mrows.shape[0]):
                    c = c + jnp.where(mrows[o, j] == j + d, mweights[o, j], 0.0)
                coef[j, d] = c
            else:
                c = coef[j, d]
            term = c * win[e, j + d]
            g = term if g is None else g + term
        return halves(jnp.concatenate([res, x, g, jnp.zeros_like(g)], axis=0))

    def wait_rest(c):
        load(1, f_hbm, fs, c).wait()
        load(2, d_hbm, ds, c).wait()

    def take_rest(c):
        rows = pl.ds(pl.multiple_of(c * CHUNK, CHUNK), CHUNK)
        for g in range(order // 8):
            gr = pl.ds(g * 8, 8)
            F[rows, gr, :] = jnp.swapaxes(fs[gr, rows, :], 0, 1)
        for g in range(ni // 8):
            gr = pl.ds(g * 8, 8)
            D[rows, gr, :] = jnp.swapaxes(ds[gr, rows, :], 0, 1)

    def advance(now, later):
        if later is not None and later[0] == 0:
            take_rest(later[1])
        news = []
        for t in range(CHUNK):
            if later is not None:
                e, c, slot = later
                hi, lo = right_hand(e, c * CHUNK + t)
                RH[slot][t] = hi
                RL[slot][t] = lo
            if now is not None:
                e, c, slot = now
                j = c * CHUNK + t
                o = jnp.dot(wcat[...], RH[slot][t], preferred_element_type=jnp.float32)
                o2 = jnp.dot(wcat[0:order, :], RL[slot][t], preferred_element_type=jnp.float32)
                new = S[e % 2][j + 1] + (o[0:order] + (o[order:] + o2))
                if e + 1 < SWEEPS:
                    S[(e + 1) % 2][j + 1] = new
                    put_plane(e + 1, j, new)
                else:
                    news.append(new)
        if now is None:
            return
        e, c, slot = now
        if e + 1 < SWEEPS:
            sister(e + 1, c).start()
        else:
            rows = pl.ds(pl.multiple_of(c * CHUNK, CHUNK), CHUNK)
            for g in range(0, order, 8):
                block = jnp.stack([new[g : g + 8] for new in news])
                xs[g : g + 8, rows, :] = jnp.swapaxes(block, 0, 1)
            store(c).start()

    def ghost_row(e, f):
        picked = recv[e, 0, 1 - f]
        for bit in range(1, BITS):
            picked = jnp.where(pbit[0, 0] == bit, recv[e, bit, 1 - f], picked)
        both = jnp.concatenate(halves(picked), axis=0)
        both = jnp.dot(both, turn_k[...], preferred_element_type=jnp.float32)
        parts = both.astype(jnp.bfloat16)
        swap = turn_i[...]
        first = jnp.dot(swap, parts[0:order], preferred_element_type=jnp.float32)
        second = jnp.dot(swap, parts[order:], preferred_element_type=jnp.float32)
        S[e % 2][0 if f == 0 else nj + 1] = first + second

    def chunk_at(pos):
        return jnp.where(
            pos < nch - 4,
            pos + 2,
            jnp.where(pos < nch - 3, 1, jnp.where(pos < nch - 2, nch - 2, 0)),
        )

    def ready(e, pos):
        @pl.when(pos < nch - 4)
        def _():
            sister(e, pos + 3).wait_recv()

        @pl.when(pos == nch - 4)
        def _():
            sister(e, 0).wait_recv()

        @pl.when(pos == nch - 3)
        def _():
            sister(e, nch - 1).wait_recv()

        @pl.when(pos == nch - 2)
        def _():
            for f in range(2):
                for bit in range(BITS):
                    face(e, bit, f).wait()
                edge(e, f).wait()
            for f in range(2):
                ghost_row(e, f)

        if e == 0:
            wait_rest(chunk_at(pos))

    def first_ready(e):
        for c in (1, 2, 3):
            sister(e, c).wait_recv()
        if e == 0:
            wait_rest(2)

    first_ready(0)
    advance(None, (0, 2, 0))
    for e in range(SWEEPS):

        def two(it, carry):
            for half in range(2):
                pos = 2 * it + half
                ready(e, pos + 1)
                advance((e, chunk_at(pos), half), (e, chunk_at(pos + 1), 1 - half))
            return carry

        lax.fori_loop(0, nch // 2 - 1, two, 0)
        if e == 0:
            wait_rest(nch - 1)
        advance((e, 0, 0), (e, nch - 1, 1))
        if e + 1 < SWEEPS:
            send_ends(e + 1, 0)
            first_ready(e + 1)
            advance((e, nch - 1, 1), (e + 1, 2, 0))
            send_ends(e + 1, 1)
        else:
            advance((e, nch - 1, 1), None)

        def sent(c, carry):
            sister(e, c).wait_send()
            return carry

        lax.fori_loop(0, nch, sent, 0)

    def finish(c, carry):
        store(c).wait()
        return carry

    lax.fori_loop(0, nch, finish, 0)


def body(nblk, state, forcing, stiffness, advection, inverse, mrows, mweights, pbit, tcode):
    _, _, nv, ni, nj, nk = state.shape
    order = nv * ni
    nch = nj // CHUNK
    f32 = jnp.float32
    anywhere = pl.BlockSpec(memory_space=pl.ANY)
    smem = pl.BlockSpec(memory_space=pltpu.SMEM)
    vmem = pl.BlockSpec(memory_space=pltpu.VMEM)
    dma = pltpu.SemaphoreType.DMA
    out = pl.pallas_call(
        functools.partial(kernel, nblk, nv, ni),
        out_shape=jax.ShapeDtypeStruct((order, nj, nk), f32),
        in_specs=[anywhere] * 3 + [smem, vmem, smem, smem, smem, smem],
        out_specs=anywhere,
        scratch_shapes=[
            pltpu.VMEM((nj + 2, order, nk), f32),
            pltpu.VMEM((nj + 2, order, nk), f32),
            pltpu.VMEM((nj, order, nk), f32),
            pltpu.VMEM((nj, ni, nk), f32),
            pltpu.VMEM((order, nj, nk), f32),
            pltpu.VMEM((order, nj, nk), f32),
            pltpu.VMEM((ni, nj, nk), f32),
            pltpu.VMEM((SWEEPS, BITS, 2, order, nk), f32),
            pltpu.VMEM((SWEEPS, nj + 2 * HW, 8, nk), f32),
            pltpu.VMEM((SWEEPS, nj, 8, nk), f32),
            pltpu.VMEM((2 * order, 2 * order + 16), jnp.bfloat16),
            pltpu.VMEM((order, order), jnp.bfloat16),
            pltpu.VMEM((nk, nk), jnp.bfloat16),
            pltpu.SMEM((nj, 2 * HW + 1), f32),
        ]
        + [pltpu.VMEM((CHUNK, 2 * order + 16, nk), jnp.bfloat16)] * 4
        + [
            dma((3, nch)),
            dma((nch,)),
            dma((SWEEPS, BITS, 2)),
            dma((SWEEPS, BITS, 2)),
            dma((SWEEPS, nch)),
            dma((SWEEPS, nch)),
            dma((SWEEPS, 2)),
            dma((SWEEPS, 2)),
        ],
        compiler_params=pltpu.CompilerParams(
            collective_id=0, has_side_effects=True, vmem_limit_bytes=56 * 1024 * 1024
        ),
        cost_estimate=pl.CostEstimate(
            flops=SWEEPS * 6 * order * (2 * order + 16) * nj * nk,
            bytes_accessed=4 * (3 * nv + 1) * ni * nj * nk,
            transcendentals=0,
        ),
    )(
        state.reshape(order, nj, nk),
        forcing.reshape(order, nj, nk),
        stiffness.reshape(ni, nj, nk),
        advection.transpose(0, 2, 1, 3)[0],
        inverse[0, 0],
        mrows[0, 0].T,
        mweights[0, 0].T,
        pbit,
        tcode,
    )
    return out.reshape(state.shape)


def solution(mesh):
    return jax.shard_map(
        functools.partial(body, mesh.shape["blk"]),
        mesh=mesh,
        in_specs=(
            P("row", "blk", None, None, None, None),
            P("row", "blk", None, None, None, None),
            P("row", "blk", None, None, None),
            P("row", "blk", None, None),
            P("row", "blk", None, None),
            P("row", "blk", None, None),
            P("row", "blk", None, None),
            P("row", "blk"),
            P("row", "blk"),
        ),
        out_specs=P("row", "blk", None, None, None, None),
        check_vma=False,
    )
```

```python
import functools

import jax
import jax.numpy as jnp
from jax import lax
from jax.experimental import pallas as pl
from jax.experimental.pallas import tpu as pltpu
from jax.sharding import PartitionSpec as P

HW = 2
SWEEPS = 3
BITS = 3
CHUNK = 8
MESH = pl.DeviceIdType.MESH
EXACT = lax.Precision.HIGHEST


def line_matrix(inverse_ref, jacobian_ref, rotor, nv, ni):
    order = nv * ni
    width = 2 * order + 16
    row = lax.broadcasted_iota(jnp.int32, (order, width), 0)
    col = lax.broadcasted_iota(jnp.int32, (order, width), 1)
    v, i = row // ni, row % ni
    identity = col == row
    in_state = (col >= order) & (col < 2 * order)
    cs = col - order
    w, ic = cs // ni, cs % ni
    ghost = cs - order
    is_ghost = col >= 2 * order
    rotor_m = jnp.broadcast_to(rotor, (order, width))
    top, bottom = i == ni - 1, i == 0
    stator_m = jnp.logical_not(rotor_m)
    up = (in_state & ((ic == i + 1) | (stator_m & top & (ic == ni - 1)))) | (is_ghost & rotor_m & top)
    down = (in_state & ((ic == i - 1) | (rotor_m & bottom & (ic == 0)))) | (
        is_ghost & stator_m & bottom
    )
    upf = jnp.where(up, 1.0, 0.0)
    downf = jnp.where(down, 1.0, 0.0)
    wv = jnp.where(is_ghost, ghost, w)
    coupling = jnp.zeros((order, width), jnp.float32)
    for a in range(nv):
        for b in range(nv):
            coupling = jnp.where((v == a) & (wv == b), jacobian_ref[a, 0, b], coupling)
    same = jnp.where(v == wv, 1.0, 0.0)
    m = jnp.where(identity, 1.0, 0.0) + same * (upf + downf) - 0.5 * coupling * (upf - downf)
    return jnp.dot(inverse_ref[...], m, precision=EXACT, preferred_element_type=jnp.float32)


def kernel(
    nblk,
    nv,
    ni,
    x_hbm,
    f_hbm,
    d_hbm,
    jac,
    inverse,
    mrows,
    mweights,
    pbit,
    tcode,
    out_hbm,
    S0,
    S1,
    F,
    D,
    xs,
    fs,
    ds,
    recv,
    win,
    plane,
    wcat,
    turn_i,
    turn_k,
    coef,
    RH0,
    RH1,
    RL0,
    RL1,
    in_sem,
    out_sem,
    face_send,
    face_recv,
    sis_send,
    sis_recv,
    edge_send,
    edge_recv,
):
    order = nv * ni
    S, RH, RL = (S0, S1), (RH0, RH1), (RL0, RL1)
    nj, nk = x_hbm.shape[1], x_hbm.shape[2]
    nch = nj // CHUNK
    r = lax.axis_index("row")
    b = lax.axis_index("blk")
    rotor = r == 0
    other = 1 - r
    nxt = lax.rem(b + 1, nblk)
    prv = lax.rem(b + nblk - 1, nblk)
    partners = []
    for bit in range(BITS):
        s = 1 << bit
        partners.append(b + s * (1 - 2 * ((b // s) % 2)))

    def load(which, src, dst, c):
        rows = pl.ds(pl.multiple_of(c * CHUNK, CHUNK), CHUNK)
        return pltpu.make_async_copy(src.at[:, rows, :], dst.at[:, rows, :], in_sem.at[which, c])

    def store(c):
        lines = S[SWEEPS % 2].at[pl.ds(c * CHUNK + 1, CHUNK)]
        return pltpu.make_async_copy(lines, out_hbm.at[pl.ds(c * CHUNK, CHUNK)], out_sem.at[c])

    for c in [0, nch - 1] + list(range(1, nch - 1)):
        load(0, x_hbm, xs, c).start()
    for c in list(range(2, nch - 2)) + [1, nch - 2, 0, nch - 1]:
        load(1, f_hbm, fs, c).start()
        load(2, d_hbm, ds, c).start()

    barrier = pltpu.get_barrier_semaphore()
    friends = [(other, b), (other, prv), (other, nxt)] + [(r, p) for p in partners]
    for friend in friends:
        pl.semaphore_signal(barrier, inc=1, device_id=friend, device_id_type=MESH)

    wfull = line_matrix(inverse, jac, rotor, nv, ni)
    whi = wfull.astype(jnp.bfloat16)
    wlo = (wfull - whi.astype(jnp.float32)).astype(jnp.bfloat16)
    wcat[0:order, :] = whi
    wcat[order : 2 * order, :] = wlo
    code = tcode[0, 0]
    ra = lax.broadcasted_iota(jnp.int32, (order, order), 0)
    ca = lax.broadcasted_iota(jnp.int32, (order, order), 1)
    turned = ra // ni * ni + (ni - 1 - ra % ni)
    chosen = jnp.where(code % 2 == 1, turned, ra)
    turn_i[...] = jnp.where(ca == chosen, 1.0, 0.0).astype(jnp.bfloat16)
    rk = lax.broadcasted_iota(jnp.int32, (nk, nk), 0)
    ck = lax.broadcasted_iota(jnp.int32, (nk, nk), 1)
    chosen_k = jnp.where(code // 2 == 1, nk - 1 - rk, rk)
    turn_k[...] = jnp.where(ck == chosen_k, 1.0, 0.0).astype(jnp.bfloat16)

    plane[...] = jnp.zeros_like(plane)

    def face(e, bit, f, first=0, count=None):
        lines = pl.ds(first, order if count is None else count)
        return pltpu.make_async_remote_copy(
            src_ref=S[e % 2].at[1 if f == 0 else nj, lines],
            dst_ref=recv.at[e, bit, f, lines],
            send_sem=face_send.at[e, bit, f],
            recv_sem=face_recv.at[e, bit, f],
            device_id=(r, partners[bit]),
            device_id_type=MESH,
        )

    def sister(e, c):
        return pltpu.make_async_remote_copy(
            src_ref=plane.at[e, pl.ds(c * CHUNK, CHUNK)],
            dst_ref=win.at[e, pl.ds(HW + c * CHUNK, CHUNK)],
            send_sem=sis_send.at[e, c],
            recv_sem=sis_recv.at[e, c],
            device_id=(other, b),
            device_id_type=MESH,
        )

    def edge(e, f):
        return pltpu.make_async_remote_copy(
            src_ref=plane.at[e, pl.ds(nj - HW if f == 0 else 0, HW)],
            dst_ref=win.at[e, pl.ds(0 if f == 0 else nj + HW, HW)],
            send_sem=edge_send.at[e, f],
            recv_sem=edge_recv.at[e, f],
            device_id=(other, nxt if f == 0 else prv),
            device_id_type=MESH,
        )

    def put_plane(e, j, new):
        for v in range(nv):
            last = new[v * ni + ni - 1 : v * ni + ni]
            first = new[v * ni : v * ni + 1]
            plane[e, j, v : v + 1, :] = jnp.where(rotor, last, first)

    def send_ends(e, f):
        edge(e, 1 - f).start()
        for first in range(0, order, 24):
            for bit in range(BITS):
                face(e, bit, f, first, 24).start()

    def take_state(c):
        load(0, x_hbm, xs, c).wait()
        j0 = pl.multiple_of(c * CHUNK, CHUNK)

        def group(g, carry):
            gr = pl.ds(pl.multiple_of(g * 8, 8), 8)
            S0[pl.ds(j0 + 1, CHUNK), gr, :] = jnp.swapaxes(xs[gr, pl.ds(j0, CHUNK), :], 0, 1)
            return carry

        lax.fori_loop(0, order // 8, group, 0, unroll=6)

        for jj in range(CHUNK):
            put_plane(0, j0 + jj, S0[j0 + jj + 1])

    take_state(0)
    pl.semaphore_wait(barrier, len(friends))
    sister(0, 0).start()
    send_ends(0, 0)
    take_state(nch - 1)
    sister(0, nch - 1).start()
    send_ends(0, 1)

    def middle(c, carry):
        take_state(c)
        sister(0, c).start()
        return carry

    lax.fori_loop(1, nch - 1, middle, 0)

    lane = lax.broadcasted_iota(jnp.int32, (order, 128), 1)

    def halves(value):
        hi = value.astype(jnp.bfloat16)
        return hi, (value - hi.astype(jnp.float32)).astype(jnp.bfloat16)

    def span_sum(x):
        tiles = [x[:, t : t + 128] for t in range(0, nk, 128)]
        after = [pltpu.roll(t, 1, 1) for t in tiles]
        ahead = [pltpu.roll(t, 127, 1) for t in tiles]
        sums = []
        for t in range(len(tiles)):
            from_left = after[t - 1] if t else 0.0
            from_right = ahead[t + 1] if t + 1 < len(tiles) else 0.0
            below = jnp.where(lane == 0, from_left, after[t])
            above = jnp.where(lane == 127, from_right, ahead[t])
            sums.append(below + above)
        return jnp.concatenate(sums, axis=1)

    def right_hand(e, j):
        src = S[e % 2]
        x = src[j + 1]
        diag = jnp.concatenate([D[j]] * nv, axis=0)
        near = (src[j] + src[j + 2]) + span_sum(x)
        res = F[j] - diag * x + near
        g = None
        for d in range(2 * HW + 1):
            if e == 0:
                c = jnp.float32(0.0)
                for o in range(mrows.shape[0]):
                    c = c + jnp.where(mrows[o, j] == j + d, mweights[o, j], 0.0)
                coef[j, d] = c
            else:
                c = coef[j, d]
            term = c * win[e, j + d]
            g = term if g is None else g + term
        return halves(jnp.concatenate([res, x, g, jnp.zeros_like(g)], axis=0))

    def wait_rest(c):
        load(1, f_hbm, fs, c).wait()
        load(2, d_hbm, ds, c).wait()

    def take_rest(c):
        rows = pl.ds(pl.multiple_of(c * CHUNK, CHUNK), CHUNK)
        for g in range(order // 8):
            gr = pl.ds(g * 8, 8)
            F[rows, gr, :] = jnp.swapaxes(fs[gr, rows, :], 0, 1)
        for g in range(ni // 8):
            gr = pl.ds(g * 8, 8)
            D[rows, gr, :] = jnp.swapaxes(ds[gr, rows, :], 0, 1)

    def advance(now, later):
        if later is not None and later[0] == 0:
            take_rest(later[1])
        for t in range(CHUNK):
            if later is not None:
                e, c, slot = later
                hi, lo = right_hand(e, c * CHUNK + t)
                RH[slot][t] = hi
                RL[slot][t] = lo
            if now is not None:
                e, c, slot = now
                j = c * CHUNK + t
                o = jnp.dot(wcat[...], RH[slot][t], preferred_element_type=jnp.float32)
                o2 = jnp.dot(wcat[0:order, :], RL[slot][t], preferred_element_type=jnp.float32)
                new = S[e % 2][j + 1] + (o[0:order] + (o[order:] + o2))
                S[(e + 1) % 2][j + 1] = new
                if e + 1 < SWEEPS:
                    put_plane(e + 1, j, new)
        if now is None:
            return
        e, c, slot = now
        if e + 1 < SWEEPS:
            sister(e + 1, c).start()
        else:
            store(c).start()

    def ghost_row(e, f):
        picked = recv[e, 0, 1 - f]
        for bit in range(1, BITS):
            picked = jnp.where(pbit[0, 0] == bit, recv[e, bit, 1 - f], picked)
        both = jnp.concatenate(halves(picked), axis=0)
        both = jnp.dot(both, turn_k[...], preferred_element_type=jnp.float32)
        parts = both.astype(jnp.bfloat16)
        swap = turn_i[...]
        first = jnp.dot(swap, parts[0:order], preferred_element_type=jnp.float32)
        second = jnp.dot(swap, parts[order:], preferred_element_type=jnp.float32)
        S[e % 2][0 if f == 0 else nj + 1] = first + second

    def chunk_at(pos):
        return jnp.where(
            pos < nch - 4,
            pos + 2,
            jnp.where(pos < nch - 3, 1, jnp.where(pos < nch - 2, nch - 2, 0)),
        )

    def ready(e, pos):
        @pl.when(pos < nch - 4)
        def _():
            sister(e, pos + 3).wait_recv()

        @pl.when(pos == nch - 4)
        def _():
            sister(e, 0).wait_recv()

        @pl.when(pos == nch - 3)
        def _():
            sister(e, nch - 1).wait_recv()

        @pl.when(pos == nch - 2)
        def _():
            for f in range(2):
                for bit in range(BITS):
                    face(e, bit, f).wait()
                edge(e, f).wait()
            for f in range(2):
                ghost_row(e, f)

        if e == 0:
            wait_rest(chunk_at(pos))

    def first_ready(e):
        for c in (1, 2, 3):
            sister(e, c).wait_recv()
        if e == 0:
            wait_rest(2)

    first_ready(0)
    advance(None, (0, 2, 0))
    for e in range(SWEEPS):

        def two(it, carry):
            for half in range(2):
                pos = 2 * it + half
                ready(e, pos + 1)
                advance((e, chunk_at(pos), half), (e, chunk_at(pos + 1), 1 - half))
            return carry

        lax.fori_loop(0, nch // 2 - 1, two, 0)
        if e == 0:
            wait_rest(nch - 1)
        advance((e, 0, 0), (e, nch - 1, 1))
        if e + 1 < SWEEPS:
            send_ends(e + 1, 0)
            first_ready(e + 1)
            advance((e, nch - 1, 1), (e + 1, 2, 0))
            send_ends(e + 1, 1)
        else:
            advance((e, nch - 1, 1), None)

        def sent(c, carry):
            sister(e, c).wait_send()
            return carry

        lax.fori_loop(0, nch, sent, 0)

    def finish(c, carry):
        store(c).wait()
        return carry

    lax.fori_loop(0, nch, finish, 0)


def lines_to_cells(lines, cells):
    for g in range(0, lines.shape[1], 8):
        cells[g : g + 8] = jnp.swapaxes(lines[:, g : g + 8, :], 0, 1)


def body(nblk, state, forcing, stiffness, advection, inverse, mrows, mweights, pbit, tcode):
    _, _, nv, ni, nj, nk = state.shape
    order = nv * ni
    nch = nj // CHUNK
    f32 = jnp.float32
    anywhere = pl.BlockSpec(memory_space=pl.ANY)
    smem = pl.BlockSpec(memory_space=pltpu.SMEM)
    vmem = pl.BlockSpec(memory_space=pltpu.VMEM)
    dma = pltpu.SemaphoreType.DMA
    out = pl.pallas_call(
        functools.partial(kernel, nblk, nv, ni),
        out_shape=jax.ShapeDtypeStruct((nj, order, nk), f32),
        in_specs=[anywhere] * 3 + [smem, vmem, smem, smem, smem, smem],
        out_specs=anywhere,
        scratch_shapes=[
            pltpu.VMEM((nj + 2, order, nk), f32),
            pltpu.VMEM((nj + 2, order, nk), f32),
            pltpu.VMEM((nj, order, nk), f32),
            pltpu.VMEM((nj, ni, nk), f32),
            pltpu.VMEM((order, nj, nk), f32),
            pltpu.VMEM((order, nj, nk), f32),
            pltpu.VMEM((ni, nj, nk), f32),
            pltpu.VMEM((SWEEPS, BITS, 2, order, nk), f32),
            pltpu.VMEM((SWEEPS, nj + 2 * HW, 8, nk), f32),
            pltpu.VMEM((SWEEPS, nj, 8, nk), f32),
            pltpu.VMEM((2 * order, 2 * order + 16), jnp.bfloat16),
            pltpu.VMEM((order, order), jnp.bfloat16),
            pltpu.VMEM((nk, nk), jnp.bfloat16),
            pltpu.SMEM((nj, 2 * HW + 1), f32),
        ]
        + [pltpu.VMEM((CHUNK, 2 * order + 16, nk), jnp.bfloat16)] * 4
        + [
            dma((3, nch)),
            dma((nch,)),
            dma((SWEEPS, BITS, 2)),
            dma((SWEEPS, BITS, 2)),
            dma((SWEEPS, nch)),
            dma((SWEEPS, nch)),
            dma((SWEEPS, 2)),
            dma((SWEEPS, 2)),
        ],
        compiler_params=pltpu.CompilerParams(
            collective_id=0, has_side_effects=True, vmem_limit_bytes=56 * 1024 * 1024
        ),
        cost_estimate=pl.CostEstimate(
            flops=SWEEPS * 6 * order * (2 * order + 16) * nj * nk,
            bytes_accessed=4 * (3 * nv + 1) * ni * nj * nk,
            transcendentals=0,
        ),
    )(
        state.reshape(order, nj, nk),
        forcing.reshape(order, nj, nk),
        stiffness.reshape(ni, nj, nk),
        advection.transpose(0, 2, 1, 3)[0],
        inverse[0, 0],
        mrows[0, 0].T,
        mweights[0, 0].T,
        pbit,
        tcode,
    )
    out = pl.pallas_call(
        lines_to_cells,
        grid=(nch,),
        out_shape=jax.ShapeDtypeStruct((order, nj, nk), f32),
        in_specs=[pl.BlockSpec((CHUNK, order, nk), lambda c: (c, 0, 0))],
        out_specs=pl.BlockSpec((order, CHUNK, nk), lambda c: (0, c, 0)),
        compiler_params=pltpu.CompilerParams(vmem_limit_bytes=60 * 1024 * 1024),
        cost_estimate=pl.CostEstimate(
            flops=0, bytes_accessed=8 * order * nj * nk, transcendentals=0
        ),
    )(out)
    return out.reshape(state.shape)


def solution(mesh):
    return jax.shard_map(
        functools.partial(body, mesh.shape["blk"]),
        mesh=mesh,
        in_specs=(
            P("row", "blk", None, None, None, None),
            P("row", "blk", None, None, None, None),
            P("row", "blk", None, None, None),
            P("row", "blk", None, None),
            P("row", "blk", None, None),
            P("row", "blk", None, None),
            P("row", "blk", None, None),
            P("row", "blk"),
            P("row", "blk"),
        ),
        out_specs=P("row", "blk", None, None, None, None),
        check_vma=False,
    )
```
